32 devices in a mesh: groups: 2 (over x), expert: 8 (over z, y), dp: 2 (over core).
Axes of the slice: x: 2, y: 2, z: 4, core: 2. Of those that a mesh axis runs over, the one named last changes fastest.
Arguments:
- tokens: bfloat16 [4096, 2048], P(('groups', 'expert', 'dp')), parts along dimension 0, may hold values from -6 to 6
- routes: int32 [4096, 8], P(('groups', 'expert', 'dp')), parts along dimension 0, may hold values from 0 to 15, all different within a row; in each aligned block of 128 rows (0 to 127, 128 to 255, ...) at most 96 rows name the same one
- gate_levels: int32 [4096, 8], P(('groups', 'expert', 'dp')), parts along dimension 0, may hold values from 1 to 15
- w_gate: bfloat16 [16, 2048, 768], P(('expert', 'dp')), may hold values from -0.125 to 0.125
- w_up: bfloat16 [16, 2048, 768], P(('expert', 'dp')), may hold values from -0.125 to 0.125
- w_down: bfloat16 [16, 768, 2048], P(('expert', 'dp')), may hold values from -0.21875 to 0.21875
Outputs:
- mixed: bfloat16 [4096, 2048], P(('groups', 'expert', 'dp')), parts along dimension 0
The draws below stay inside these ranges and needn't reach their ends.
There are 2 independent parts, one for each index of `groups`. The reference program is written for one: setup_inputs(seed, part) draws one part's arguments, and reference() takes and returns one part's arrays. A program takes and returns all parts, laid end to end along the dimension named above; an argument that names none is the same for every part. Nothing has to cross between parts.
Inputs may be any that keep to these rules, and one draw needn't show every extreme that they name: `routes`: among the 128 rows of one device, each expert is named by at most 96 rows; in every draw some device's rows name some expert exactly 96 times.
All inputs are finite; a program needn't handle non-finite values.
Results may differ from the reference program's by a relative error of at most 0.0057.
Values may be sent and summed in bfloat16 or wider, within the bound.
A program may use at most 64 MiB of HBM per device.

```python
import math
import jax
import jax.numpy as jnp
import numpy as np
from jax import lax

D = 2048
H = 768
TOP = 8
TOK_DEV = 128
EXPERTS = 16
CAP = 96
TOKENS = 2048
N_EXPERT = 8
N_DP = 2


def plant(result, stream_key, low, largest):
    place = [jax.random.randint(jax.random.fold_in(stream_key, axis), (), 0, length) for axis, length in enumerate(result.shape)]
    main_axis = result.shape.index(max(result.shape))
    neighbour = place[:main_axis] + [(place[main_axis] + 1) % result.shape[main_axis]] + place[main_axis + 1:]
    return result.at[tuple(place)].set(low).at[tuple(neighbour)].set(largest)


def block_scale(rng, dims, shards, least, largest):
    def one(axis_at, shards_of):
        draws = jax.random.uniform(jax.random.fold_in(jax.random.fold_in(rng, 6), axis_at), (shards_of,), jnp.float32, least / len(shards), largest / len(shards))
        return jnp.repeat(jnp.exp(draws), dims[axis_at] // shards_of).reshape((-1,) + (1,) * (len(dims) - axis_at - 1))

    gain = one(*shards[0])
    for cut in shards[1:]:
        gain = gain * one(*cut)
    return gain


def assign_block(own_key, own, number, rows, number_of, top, reach, slope):
    sequence = jax.random.permutation(own_key, number_of)
    heavy_load, usual = load_shares(number_of, rows * top, reach, slope, True), load_shares(number_of, rows * top, reach, slope, False)
    places = jnp.arange(number_of)

    def named(sizes, rotation):
        used = int((sizes > 0).sum())
        fixed = max(1, used // 4)
        shifted = fixed + (places - fixed + rotation * (used - fixed)) % max(1, number_of - fixed)
        return jnp.zeros((number_of,), jnp.int32).at[sequence[jnp.where(places < fixed, places, shifted)]].set(jnp.asarray(sizes, jnp.int32))

    sizes = jnp.where(number % 4 == 0, named(heavy_load, number // 4), named(usual, number - number // 4 - 1))
    mixed = jax.random.permutation(jax.random.fold_in(own, 3), number_of)
    donor, receiver = mixed[0:number_of // 2 * 2:2], mixed[1:number_of // 2 * 2:2]
    room = jnp.minimum(sizes[donor] - 1, reach - sizes[receiver]) // 2
    room = jnp.where((donor == sequence[0]) | (receiver == sequence[0]) | (sizes[receiver] == 0), 0, jnp.maximum(room, 0))
    shifted = jax.random.randint(jax.random.fold_in(own, 4), (number_of // 2,), 0, 1 << 20) % (room + 1)
    sizes = sizes.at[donor].add(-shifted).at[receiver].add(shifted)
    members = jnp.searchsorted(jnp.cumsum(sizes), jnp.arange(rows * top), side="right").astype(jnp.int32)
    table = members.reshape(top, rows).T
    table = table[jax.random.permutation(jax.random.fold_in(own, 1), rows)]
    rotation = jax.random.randint(jax.random.fold_in(own, 2), (rows, 1), 0, top)
    return jnp.take_along_axis(table, (jnp.arange(top)[None, :] + rotation) % top, axis=1)


def load_shares(number_of, total, limit, skew, full):
    loads = [(1 << 20) // math.isqrt(standing ** skew) + 1 for standing in range(1, number_of + 1)]
    largest = limit if full else min(limit, max(-(-total // number_of), total * loads[0] // sum(loads)))
    least = 1 if total - largest >= number_of - 1 else 0
    given, spare = [largest] + [least] * (number_of - 1), total - largest - least * (number_of - 1)
    while spare > 0:
        movable = [i for i in range(1, number_of) if given[i] < largest] or [i for i in range(1, number_of) if given[i] < limit]
        pool, left = sum([loads[i] for i in movable]), spare
        for i in movable:
            extra = min(limit - given[i], max(1, left * loads[i] // pool), spare)
            given[i] = given[i] + extra
            spare = spare - extra
    return np.array(given)


def noise(stream_key, shape, spread, limit, shards=(), kind=jnp.bfloat16):
    entries = spread * jax.random.normal(stream_key, shape, jnp.float32)
    if shards:
        entries = entries * block_scale(stream_key, shape, shards, -0.22, 0.18)
    return jnp.clip(entries, -limit, limit).astype(kind)


def setup_inputs(seed: int = 0, part: int = 0) -> dict:
    seeds = jax.random.split(jax.random.key(seed), 7)
    own_keys = jax.random.split(jax.random.fold_in(seeds[6], part), 7)
    tokens = noise(own_keys[0], (TOKENS, D), 1.0, 6.0, ((0, 16),))
    routes_keys = jax.random.split(jax.random.fold_in(own_keys[1], 1), TOKENS // TOK_DEV)
    routes_turns = jax.random.permutation(jax.random.fold_in(own_keys[1], 3), TOKENS // TOK_DEV)
    routes = jax.vmap(lambda own, number: assign_block(jax.random.fold_in(own_keys[1], 2), own, number, TOK_DEV, EXPERTS, TOP, CAP, 2))(routes_keys, routes_turns).reshape((TOKENS, TOP))
    gate_levels = plant(jax.random.randint(own_keys[2], (TOKENS, TOP), 1, 16), jax.random.fold_in(own_keys[2], 1), 1, 15).astype(jnp.int32)
    w_gate = noise(seeds[3], (EXPERTS, D, H), D ** -0.5, 0.125, ((0, 16),))
    w_up = noise(seeds[4], (EXPERTS, D, H), D ** -0.5, 0.125, ((0, 16),))
    w_down = noise(seeds[5], (EXPERTS, H, D), H ** -0.5, 0.21875, ((0, 16),))
    return {"tokens": tokens, "routes": routes, "gate_levels": gate_levels, "w_gate": w_gate, "w_up": w_up, "w_down": w_down}


def reference(tokens, routes, gate_levels, w_gate, w_up, w_down):
    route_list = routes.reshape(-1)
    levels = gate_levels.astype(jnp.float32)
    weights = (levels / jnp.sum(levels, axis=1, keepdims=True)).reshape(-1)
    row_max = CAP * N_EXPERT * N_DP

    def per_expert(expert_id, accumulated):
        matches = route_list == expert_id
        row_count = jnp.sum(matches.astype(jnp.int32))
        picked = jnp.nonzero(matches, size=row_max, fill_value=0)[0].astype(jnp.int32)
        is_live = jnp.arange(row_max, dtype=jnp.int32) < row_count
        owner_row = picked // TOP
        inputs = tokens[owner_row]
        gate_mat = lax.dynamic_index_in_dim(w_gate, expert_id, 0, keepdims=False)
        up_mat = lax.dynamic_index_in_dim(w_up, expert_id, 0, keepdims=False)
        down_mat = lax.dynamic_index_in_dim(w_down, expert_id, 0, keepdims=False)
        gate_act = jnp.dot(inputs, gate_mat, preferred_element_type=jnp.float32)
        up_act = jnp.dot(inputs, up_mat, preferred_element_type=jnp.float32)
        hidden = (jax.nn.silu(gate_act) * up_act).astype(jnp.bfloat16)
        produced = jnp.dot(hidden, down_mat, preferred_element_type=jnp.float32).astype(jnp.bfloat16)
        factor = jnp.where(is_live, weights[picked], 0.0)
        return accumulated.at[owner_row].add(produced.astype(weights.dtype) * factor[:, None])

    start = jnp.zeros((TOKENS, D), weights.dtype)
    accumulated = lax.fori_loop(0, EXPERTS, per_expert, start)
    return accumulated.astype(jnp.bfloat16)
```

```python
import jax
import jax.numpy as jnp
from jax import lax
from jax.sharding import PartitionSpec as P

AXES = ("expert", "dp")


def expert_part(x, factor, w_gate, w_up, w_down):
    gate_act = jnp.dot(x, w_gate, preferred_element_type=jnp.float32)
    up_act = jnp.dot(x, w_up, preferred_element_type=jnp.float32)
    hidden = (jax.nn.silu(gate_act) * up_act).astype(jnp.bfloat16)
    produced = jnp.dot(hidden, w_down, preferred_element_type=jnp.float32)
    return (produced * factor).astype(jnp.bfloat16)


def per_device(tokens, routes, gate_levels, w_gate, w_up, w_down):
    rows, width = tokens.shape
    devices = lax.axis_size("expert") * lax.axis_size("dp")
    me = lax.axis_index("expert") * lax.axis_size("dp") + lax.axis_index("dp")
    named = routes[:, :, None] == jnp.arange(devices, dtype=jnp.int32)[None, None, :]
    levels = gate_levels.astype(jnp.float32)
    weights = levels / jnp.sum(levels, axis=1, keepdims=True)
    spread = jnp.sum(jnp.where(named, weights[:, :, None], 0.0), axis=1)
    factors = lax.all_gather(spread, AXES, axis=0, tiled=False)
    mine = lax.dynamic_index_in_dim(factors, me, 2, keepdims=True)
    chunks = 2 if devices <= 16 else 8
    step = rows // chunks
    results = []
    for c in range(chunks):
        part = slice(c * step, (c + 1) * step)
        block = tokens[part]
        if devices > 16 and c > 0:
            block, _ = lax.optimization_barrier((block, results[-1]))
        x = lax.all_gather(block, AXES, axis=0, tiled=True)
        y = expert_part(x, mine[:, part].reshape(-1, 1), w_gate[0], w_up[0], w_down[0])
        results.append(lax.psum_scatter(y, AXES, scatter_dimension=0, tiled=True))
    return jnp.concatenate(results, axis=0)


def solution(mesh):
    token_spec = P(("groups", "expert", "dp"), None)
    weight_spec = P(("expert", "dp"), None, None)
    return jax.shard_map(
        per_device,
        mesh=mesh,
        in_specs=(token_spec,) * 3 + (weight_spec,) * 3,
        out_specs=token_spec,
        check_vma=False,
    )
```

```python
import functools
import jax
import jax.numpy as jnp
from jax import lax
from jax.experimental import pallas as pl
from jax.experimental.pallas import tpu as pltpu
from jax.sharding import PartitionSpec as P

AXES = ("expert", "dp")


def expert_part(x, factor, w_gate, w_up, w_down):
    gate_act = jnp.dot(x, w_gate, preferred_element_type=jnp.float32)
    up_act = jnp.dot(x, w_up, preferred_element_type=jnp.float32)
    hidden = (jax.nn.silu(gate_act) * up_act).astype(jnp.bfloat16)
    produced = jnp.dot(hidden, w_down, preferred_element_type=jnp.float32)
    return (produced * factor).astype(jnp.bfloat16)


def by_collectives(tokens, routes, gate_levels, w_gate, w_up, w_down):
    rows, width = tokens.shape
    devices = lax.axis_size("expert") * lax.axis_size("dp")
    me = lax.axis_index("expert") * lax.axis_size("dp") + lax.axis_index("dp")
    named = routes[:, :, None] == jnp.arange(devices, dtype=jnp.int32)[None, None, :]
    levels = gate_levels.astype(jnp.float32)
    weights = levels / jnp.sum(levels, axis=1, keepdims=True)
    spread = jnp.sum(jnp.where(named, weights[:, :, None], 0.0), axis=1)
    factors = lax.all_gather(spread, AXES, axis=0, tiled=False)
    mine = lax.dynamic_index_in_dim(factors, me, 2, keepdims=True)
    chunks = 2 if devices <= 16 else 8
    step = rows // chunks
    results = []
    for c in range(chunks):
        part = slice(c * step, (c + 1) * step)
        block = tokens[part]
        if devices > 16 and c > 0:
            block, _ = lax.optimization_barrier((block, results[-1]))
        x = lax.all_gather(block, AXES, axis=0, tiled=True)
        y = expert_part(x, mine[:, part].reshape(-1, 1), w_gate[0], w_up[0], w_down[0])
        results.append(lax.psum_scatter(y, AXES, scatter_dimension=0, tiled=True))
    return jnp.concatenate(results, axis=0)


LANES = 128
VMEM_ROOM = 56 * 1024 * 1024


def kernel(
    n, block_ref, gate_hbm, up_hbm, down_hbm, out_ref,
    x, w_gate, w_up, w_down, hid, own, sent, sib, run,
    load_sem, ring_send, ring_recv, pair_send, pair_recv,
    back_send, back_recv, run_send, run_recv,
):
    half_ring = n // 2
    rows, width = out_ref.shape
    piece = rows // 2
    expert = lax.axis_index("expert")
    core = lax.axis_index("dp")
    odd, rank = expert % 2, expert // 2
    place = rank + odd * (n - 1 - 2 * rank)

    def chip_at(p):
        return 2 * p + (p // half_ring) * (2 * n - 1 - 4 * p)

    right = {"expert": chip_at((place + 1) % n), "dp": core}
    left = {"expert": chip_at((place + n - 1) % n), "dp": core}
    other = {"expert": expert, "dp": 1 - core}
    ways = (right, left)
    number = expert * 2 + core

    loads = [
        pltpu.make_async_copy(src, dst, load_sem.at[i])
        for i, (src, dst) in enumerate(
            [
                (block_ref, x.at[0, pl.ds(0, rows)]),
                (gate_hbm.at[0], w_gate),
                (up_hbm.at[0], w_up),
                (down_hbm.at[0], w_down),
            ]
        )
    ]
    for load in loads:
        load.start()

    barrier = pltpu.get_barrier_semaphore()
    for device in (right, left, other):
        pl.semaphore_signal(barrier, inc=1, device_id=device, device_id_type=pl.DeviceIdType.MESH)
    pl.semaphore_wait(barrier, 3)

    def slot_of(way, step):
        return step if way == 0 else (n - step) % n

    def remote(src, dst, send, recv, device):
        return pltpu.make_async_remote_copy(
            src_ref=src, dst_ref=dst, send_sem=send, recv_sem=recv,
            device_id=device, device_id_type=pl.DeviceIdType.MESH,
        )

    def ring_copy(way, step, part):
        rows_of = pl.ds(part * piece, piece)
        return remote(
            x.at[slot_of(way, step), rows_of], x.at[slot_of(way, step + 1), rows_of],
            ring_send.at[way, step, part], ring_recv.at[way, step, part], ways[way],
        )

    def pair_copy(slot, part):
        return remote(
            x.at[slot, pl.ds(part * piece, piece)], x.at[slot, pl.ds(rows + part * piece, piece)],
            pair_send.at[slot, part], pair_recv.at[slot, part], other,
        )

    def back_copy(slot):
        return remote(sent.at[slot], sib.at[slot], back_send.at[slot], back_recv.at[slot], other)

    def run_copy(way, hop, part):
        rows_of = pl.ds(part * piece, piece)
        return remote(
            run.at[way, hop, rows_of], run.at[way, hop + 1, rows_of],
            run_send.at[way, hop, part], run_recv.at[way, hop, part], ways[way],
        )

    def travels(way, step, part):
        return step < half_ring - 1 or part == way

    def compute(slot):
        level = jnp.sum(
            jnp.where(
                lax.broadcasted_iota(jnp.int32, (2 * rows, LANES), 1) == number,
                x[slot, :, width:].astype(jnp.float32), 0.0,
            ),
            axis=1, keepdims=True,
        )

        def hidden_part(i, carry):
            cols = pl.ds(pl.multiple_of(i * 256, 256), 256)
            tokens = x[slot, :, :width]
            g = jnp.dot(tokens, w_gate[:, cols], preferred_element_type=jnp.float32)
            u = jnp.dot(tokens, w_up[:, cols], preferred_element_type=jnp.float32)
            hid[:, cols] = (g / (1.0 + jnp.exp(-g)) * u).astype(jnp.bfloat16)
            return carry

        lax.fori_loop(0, w_gate.shape[1] // 256, hidden_part, 0)

        def output_part(i, carry):
            cols = pl.ds(pl.multiple_of(i * 256, 256), 256)
            y = jnp.dot(hid[...], w_down[:, cols], preferred_element_type=jnp.float32) * level
            own[slot, :, cols] = y[:rows]
            sent[slot, :, cols] = y[rows:].astype(jnp.bfloat16)
            return carry

        lax.fori_loop(0, width // 256, output_part, 0)

    def slots_at(step):
        return [step] if step in (0, half_ring) else [step, n - step]

    def compute_step(step):
        for slot in slots_at(step):
            for part in range(2):
                pair_copy(slot, part).wait_recv()
        first, count = step, len(slots_at(step))

        def body(i, carry):
            compute(first + i * (n - 2 * step))
            return carry

        lax.fori_loop(0, count, body, 0)
        for slot in slots_at(step):
            back_copy(slot).start()

    loads[0].wait()
    for part in range(2):
        for way in range(2):
            ring_copy(way, 0, part if way == 0 else 1 - part).start()
    for part in range(2):
        pair_copy(0, part).start()
    for load in loads[1:]:
        load.wait()
    for step in range(1, half_ring + 1):
        compute_step(step - 1)
        for order in range(2):
            for way in range(2):
                part = order if way == 0 else 1 - order
                if not travels(way, step - 1, part):
                    continue
                ring_copy(way, step - 1, part).wait_recv()
                if step < half_ring and travels(way, step, part):
                    ring_copy(way, step, part).start()
                pair_copy(slot_of(way, step), part).start()
    compute_step(half_ring)

    def here(slot, part):
        rows_of = pl.ds(part * piece, piece)
        return own[slot, rows_of] + sib[slot, rows_of].astype(jnp.float32)

    def pass_on(way, hop, part, arrives):
        slot = (n - (half_ring - hop)) % n if way == 0 else half_ring - hop
        rows_of = pl.ds(part * piece, piece)
        total = here(slot, part)
        if arrives:
            run_copy(way, hop - 1, part).wait_recv()
            total = total + run[way, hop, rows_of].astype(jnp.float32)
        run[way, hop, rows_of] = total.astype(jnp.bfloat16)
        run_copy(way, hop, part).start()

    for step in range(1, half_ring):
        if step == half_ring - 1:
            for slot in slots_at(step):
                back_copy(slot).wait_recv()
    back_copy(half_ring).wait_recv()
    for way in range(2):
        pass_on(way, 0, way, False)
    for hop in range(1, half_ring):
        if hop > 1:
            for slot in slots_at(half_ring - hop):
                back_copy(slot).wait_recv()
        for order in range(2):
            for way in range(2):
                part = 1 - way if order == 0 else way
                pass_on(way, hop, part, hop > 1 or part == way)
    back_copy(0).wait_recv()
    for order in range(2):
        for way in range(2):
            part = 1 - way if order == 0 else way
            run_copy(way, half_ring - 1, part).wait_recv()
    for part in range(2):
        rows_of = pl.ds(part * piece, piece)
        total = here(0, part)
        for way in range(2):
            total = total + run[way, half_ring, rows_of].astype(jnp.float32)
        out_ref[rows_of] = total

    for way in range(2):
        for step in range(half_ring):
            for part in range(2):
                if travels(way, step, part):
                    ring_copy(way, step, part).wait_send()
        for hop in range(half_ring):
            for part in range(2):
                if hop > 0 or part == way:
                    run_copy(way, hop, part).wait_send()
    for slot in range(n):
        for part in range(2):
            pair_copy(slot, part).wait_send()
        back_copy(slot).wait_send()


def scratch_of(n, rows, width, hidden):
    half_ring = n // 2
    arrays = [
        ((n, 2 * rows, width + LANES), jnp.bfloat16),
        ((width, hidden), jnp.bfloat16),
        ((width, hidden), jnp.bfloat16),
        ((hidden, width), jnp.bfloat16),
        ((2 * rows, hidden), jnp.bfloat16),
        ((n, rows, width), jnp.float32),
        ((n, rows, width), jnp.bfloat16),
        ((n, rows, width), jnp.bfloat16),
        ((2, half_ring + 1, rows, width), jnp.bfloat16),
    ]
    total = sum(functools.reduce(lambda a, b: a * b, s) * jnp.dtype(t).itemsize for s, t in arrays)
    sems = [(4,), (2, half_ring, 2), (2, half_ring, 2), (n, 2), (n, 2), (n,), (n,),
            (2, half_ring, 2), (2, half_ring, 2)]
    shapes = [pltpu.VMEM(s, t) for s, t in arrays] + [pltpu.SemaphoreType.DMA(s) for s in sems]
    return shapes, total


def per_device(tokens, routes, gate_levels, w_gate, w_up, w_down):
    rows, width = tokens.shape
    hidden = w_gate.shape[2]
    n, cores = lax.axis_size("expert"), lax.axis_size("dp")
    shapes, total = scratch_of(n, rows, width, hidden)
    if total > VMEM_ROOM * 9 // 10 or n < 4 or n % 2 or cores != 2 or n * cores > LANES:
        return by_collectives(tokens, routes, gate_levels, w_gate, w_up, w_down)
    named = routes[:, :, None] == jnp.arange(LANES, dtype=jnp.int32)[None, None, :]
    levels = jnp.sum(jnp.where(named, gate_levels[:, :, None], 0), axis=1)
    block = jnp.concatenate([tokens, levels.astype(jnp.bfloat16)], axis=1)
    any_space = pl.BlockSpec(memory_space=pl.ANY)
    mixed = pl.pallas_call(
        functools.partial(kernel, n),
        out_shape=jax.ShapeDtypeStruct((rows, width), jnp.float32),
        in_specs=[any_space] * 4,
        out_specs=pl.BlockSpec(memory_space=pltpu.VMEM),
        scratch_shapes=shapes,
        compiler_params=pltpu.CompilerParams(
            collective_id=0, has_side_effects=True, vmem_limit_bytes=VMEM_ROOM
        ),
        cost_estimate=pl.CostEstimate(
            flops=12 * n * rows * width * hidden,
            bytes_accessed=6 * width * hidden,
            transcendentals=2 * n * rows * hidden,
        ),
    )(block, w_gate, w_up, w_down)
    shares = jnp.sum(gate_levels, axis=1, keepdims=True).astype(jnp.float32)
    return (mixed / shares).astype(jnp.bfloat16)


def solution(mesh):
    token_spec = P(("groups", "expert", "dp"), None)
    weight_spec = P(("expert", "dp"), None, None)
    return jax.shard_map(
        per_device,
        mesh=mesh,
        in_specs=(token_spec,) * 3 + (weight_spec,) * 3,
        out_specs=token_spec,
        check_vma=False,
    )
```

```python
import functools
import jax
import jax.numpy as jnp
from jax import lax
from jax.experimental import pallas as pl
from jax.experimental.pallas import tpu as pltpu
from jax.sharding import PartitionSpec as P

AXES = ("expert", "dp")


def expert_part(x, factor, w_gate, w_up, w_down):
    gate_act = jnp.dot(x, w_gate, preferred_element_type=jnp.float32)
    up_act = jnp.dot(x, w_up, preferred_element_type=jnp.float32)
    hidden = (jax.nn.silu(gate_act) * up_act).astype(jnp.bfloat16)
    produced = jnp.dot(hidden, w_down, preferred_element_type=jnp.float32)
    return (produced * factor).astype(jnp.bfloat16)


def by_collectives(tokens, routes, gate_levels, w_gate, w_up, w_down):
    rows, width = tokens.shape
    devices = lax.axis_size("expert") * lax.axis_size("dp")
    me = lax.axis_index("expert") * lax.axis_size("dp") + lax.axis_index("dp")
    named = routes[:, :, None] == jnp.arange(devices, dtype=jnp.int32)[None, None, :]
    levels = gate_levels.astype(jnp.float32)
    weights = levels / jnp.sum(levels, axis=1, keepdims=True)
    spread = jnp.sum(jnp.where(named, weights[:, :, None], 0.0), axis=1)
    factors = lax.all_gather(spread, AXES, axis=0, tiled=False)
    mine = lax.dynamic_index_in_dim(factors, me, 2, keepdims=True)
    chunks = 2 if devices <= 16 else 8
    step = rows // chunks
    results = []
    for c in range(chunks):
        part = slice(c * step, (c + 1) * step)
        block = tokens[part]
        if devices > 16 and c > 0:
            block, _ = lax.optimization_barrier((block, results[-1]))
        x = lax.all_gather(block, AXES, axis=0, tiled=True)
        y = expert_part(x, mine[:, part].reshape(-1, 1), w_gate[0], w_up[0], w_down[0])
        results.append(lax.psum_scatter(y, AXES, scatter_dimension=0, tiled=True))
    return jnp.concatenate(results, axis=0)


LANES = 128
VMEM_ROOM = 56 * 1024 * 1024


def kernel(
    n, token_hbm, level_hbm, gate_hbm, up_hbm, down_hbm, out_ref,
    x, w_gate, w_up, w_down, hid, own, sent, sib, run,
    load_sem, ring_send, ring_recv, pair_send, pair_recv,
    back_send, back_recv, run_send, run_recv,
):
    half_ring = n // 2
    rows, width = out_ref.shape
    piece = rows // 2
    expert = lax.axis_index("expert")
    core = lax.axis_index("dp")
    odd, rank = expert % 2, expert // 2
    place = rank + odd * (n - 1 - 2 * rank)

    def chip_at(p):
        return 2 * p + (p // half_ring) * (2 * n - 1 - 4 * p)

    right = {"expert": chip_at((place + 1) % n), "dp": core}
    left = {"expert": chip_at((place + n - 1) % n), "dp": core}
    other = {"expert": expert, "dp": 1 - core}
    ways = (right, left)
    number = expert * 2 + core

    loads = [
        pltpu.make_async_copy(src, dst, load_sem.at[i])
        for i, (src, dst) in enumerate(
            [
                (token_hbm, x.at[0, pl.ds(0, rows), pl.ds(0, width)]),
                (level_hbm, x.at[0, pl.ds(0, rows), pl.ds(width, LANES)]),
                (gate_hbm.at[0], w_gate),
                (up_hbm.at[0], w_up),
                (down_hbm.at[0], w_down),
            ]
        )
    ]
    for load in loads:
        load.start()

    barrier = pltpu.get_barrier_semaphore()
    for device in (right, left, other):
        pl.semaphore_signal(barrier, inc=1, device_id=device, device_id_type=pl.DeviceIdType.MESH)
    pl.semaphore_wait(barrier, 3)

    def slot_of(way, step):
        return step if way == 0 else (n - step) % n

    def remote(src, dst, send, recv, device):
        return pltpu.make_async_remote_copy(
            src_ref=src, dst_ref=dst, send_sem=send, recv_sem=recv,
            device_id=device, device_id_type=pl.DeviceIdType.MESH,
        )

    def ring_copy(way, step, part):
        rows_of = pl.ds(part * piece, piece)
        return remote(
            x.at[slot_of(way, step), rows_of], x.at[slot_of(way, step + 1), rows_of],
            ring_send.at[way, step, part], ring_recv.at[way, step, part], ways[way],
        )

    def pair_copy(slot, part):
        return remote(
            x.at[slot, pl.ds(part * piece, piece)], x.at[slot, pl.ds(rows + part * piece, piece)],
            pair_send.at[slot, part], pair_recv.at[slot, part], other,
        )

    def back_copy(slot):
        return remote(sent.at[slot], sib.at[slot], back_send.at[slot], back_recv.at[slot], other)

    def run_copy(way, hop, part):
        rows_of = pl.ds(part * piece, piece)
        return remote(
            run.at[way, hop, rows_of], run.at[way, hop + 1, rows_of],
            run_send.at[way, hop, part], run_recv.at[way, hop, part], ways[way],
        )

    def travels(way, step, part):
        return step < half_ring - 1 or part == way

    def compute(slot):
        level = jnp.sum(
            jnp.where(
                lax.broadcasted_iota(jnp.int32, (2 * rows, LANES), 1) == number,
                x[slot, :, width:].astype(jnp.float32), 0.0,
            ),
            axis=1, keepdims=True,
        )

        def hidden_part(i, carry):
            cols = pl.ds(pl.multiple_of(i * 256, 256), 256)
            tokens = x[slot, :, :width]
            g = jnp.dot(tokens, w_gate[:, cols], preferred_element_type=jnp.float32)
            u = jnp.dot(tokens, w_up[:, cols], preferred_element_type=jnp.float32)
            hid[:, cols] = (g / (1.0 + jnp.exp(-g)) * u).astype(jnp.bfloat16)
            return carry

        lax.fori_loop(0, w_gate.shape[1] // 256, hidden_part, 0, unroll=True)

        def output_part(i, carry):
            cols = pl.ds(pl.multiple_of(i * 256, 256), 256)
            y = jnp.dot(hid[...], w_down[:, cols], preferred_element_type=jnp.float32) * level
            own[slot, :, cols] = y[:rows]
            sent[slot, :, cols] = y[rows:].astype(jnp.bfloat16)
            return carry

        lax.fori_loop(0, width // 256, output_part, 0, unroll=True)

    def slots_at(step):
        return [step] if step in (0, half_ring) else [step, n - step]

    def compute_step(step):
        for slot in slots_at(step):
            for part in range(2):
                pair_copy(slot, part).wait_recv()
        first, count = step, len(slots_at(step))

        def body(i, carry):
            compute(first + i * (n - 2 * step))
            return carry

        lax.fori_loop(0, count, body, 0)
        for slot in slots_at(step):
            back_copy(slot).start()

    loads[0].wait()
    loads[1].wait()
    for part in range(2):
        for way in range(2):
            ring_copy(way, 0, part if way == 0 else 1 - part).start()
    for part in range(2):
        pair_copy(0, part).start()
    for load in loads[2:]:
        load.wait()
    for step in range(1, half_ring + 1):
        compute_step(step - 1)
        for order in range(2):
            for way in range(2):
                part = order if way == 0 else 1 - order
                if not travels(way, step - 1, part):
                    continue
                ring_copy(way, step - 1, part).wait_recv()
                if step < half_ring and travels(way, step, part):
                    ring_copy(way, step, part).start()
                pair_copy(slot_of(way, step), part).start()
    def here(slot, part):
        rows_of = pl.ds(part * piece, piece)
        return own[slot, rows_of] + sib[slot, rows_of].astype(jnp.float32)

    def pass_on(way, hop, part, arrives):
        slot = (n - (half_ring - hop)) % n if way == 0 else half_ring - hop
        rows_of = pl.ds(part * piece, piece)
        total = here(slot, part)
        if arrives:
            run_copy(way, hop - 1, part).wait_recv()
            total = total + run[way, hop, rows_of].astype(jnp.float32)
        run[way, hop, rows_of] = total.astype(jnp.bfloat16)
        run_copy(way, hop, part).start()

    for slot in slots_at(half_ring - 1):
        back_copy(slot).wait_recv()
    for way in range(2):
        pass_on(way, 1, 1 - way, False)
    compute_step(half_ring)
    back_copy(half_ring).wait_recv()
    for way in range(2):
        pass_on(way, 0, way, False)
    for way in range(2):
        pass_on(way, 1, way, True)
    for hop in range(2, half_ring):
        for slot in slots_at(half_ring - hop):
            back_copy(slot).wait_recv()
        for order in range(2):
            for way in range(2):
                pass_on(way, hop, 1 - way if order == 0 else way, True)
    back_copy(0).wait_recv()
    for order in range(2):
        for way in range(2):
            part = 1 - way if order == 0 else way
            run_copy(way, half_ring - 1, part).wait_recv()
    for part in range(2):
        rows_of = pl.ds(part * piece, piece)
        total = here(0, part)
        for way in range(2):
            total = total + run[way, half_ring, rows_of].astype(jnp.float32)
        levels = x[0, rows_of, width:].astype(jnp.float32)
        share = 1.0 / jnp.sum(levels, axis=1, keepdims=True)
        out_ref[rows_of] = (total * share).astype(jnp.bfloat16)

    for way in range(2):
        for step in range(half_ring):
            for part in range(2):
                if travels(way, step, part):
                    ring_copy(way, step, part).wait_send()
        for hop in range(half_ring):
            for part in range(2):
                if hop > 0 or part == way:
                    run_copy(way, hop, part).wait_send()
    for slot in range(n):
        for part in range(2):
            pair_copy(slot, part).wait_send()
        back_copy(slot).wait_send()


def scratch_of(n, rows, width, hidden):
    half_ring = n // 2
    arrays = [
        ((n, 2 * rows, width + LANES), jnp.bfloat16),
        ((width, hidden), jnp.bfloat16),
        ((width, hidden), jnp.bfloat16),
        ((hidden, width), jnp.bfloat16),
        ((2 * rows, hidden), jnp.bfloat16),
        ((n, rows, width), jnp.float32),
        ((n, rows, width), jnp.bfloat16),
        ((n, rows, width), jnp.bfloat16),
        ((2, half_ring + 1, rows, width), jnp.bfloat16),
    ]
    total = sum(functools.reduce(lambda a, b: a * b, s) * jnp.dtype(t).itemsize for s, t in arrays)
    sems = [(5,), (2, half_ring, 2), (2, half_ring, 2), (n, 2), (n, 2), (n,), (n,),
            (2, half_ring, 2), (2, half_ring, 2)]
    shapes = [pltpu.VMEM(s, t) for s, t in arrays] + [pltpu.SemaphoreType.DMA(s) for s in sems]
    return shapes, total


def per_device(tokens, routes, gate_levels, w_gate, w_up, w_down):
    rows, width = tokens.shape
    hidden = w_gate.shape[2]
    n, cores = lax.axis_size("expert"), lax.axis_size("dp")
    shapes, total = scratch_of(n, rows, width, hidden)
    if total > VMEM_ROOM * 9 // 10 or n < 4 or n % 2 or cores != 2 or n * cores > LANES:
        return by_collectives(tokens, routes, gate_levels, w_gate, w_up, w_down)
    named = routes[:, :, None] == jnp.arange(LANES, dtype=jnp.int32)[None, None, :]
    levels = jnp.sum(jnp.where(named, gate_levels[:, :, None], 0), axis=1)
    any_space = pl.BlockSpec(memory_space=pl.ANY)
    return pl.pallas_call(
        functools.partial(kernel, n),
        out_shape=jax.ShapeDtypeStruct((rows, width), jnp.bfloat16),
        in_specs=[any_space] * 5,
        out_specs=pl.BlockSpec(memory_space=pltpu.VMEM),
        scratch_shapes=shapes,
        compiler_params=pltpu.CompilerParams(
            collective_id=0, has_side_effects=True, vmem_limit_bytes=VMEM_ROOM
        ),
        cost_estimate=pl.CostEstimate(
            flops=12 * n * rows * width * hidden,
            bytes_accessed=6 * width * hidden,
            transcendentals=2 * n * rows * hidden,
        ),
    )(tokens, levels.astype(jnp.bfloat16), w_gate, w_up, w_down)


def solution(mesh):
    token_spec = P(("groups", "expert", "dp"), None)
    weight_spec = P(("expert", "dp"), None, None)
    return jax.shard_map(
        per_device,
        mesh=mesh,
        in_specs=(token_spec,) * 3 + (weight_spec,) * 3,
        out_specs=token_spec,
        check_vma=False,
    )
```

```python
import functools
import jax
import jax.numpy as jnp
from jax import lax
from jax.experimental import pallas as pl
from jax.experimental.pallas import tpu as pltpu
from jax.sharding import PartitionSpec as P

AXES = ("expert", "dp")


def expert_part(x, factor, w_gate, w_up, w_down):
    gate_act = jnp.dot(x, w_gate, preferred_element_type=jnp.float32)
    up_act = jnp.dot(x, w_up, preferred_element_type=jnp.float32)
    hidden = (jax.nn.silu(gate_act) * up_act).astype(jnp.bfloat16)
    produced = jnp.dot(hidden, w_down, preferred_element_type=jnp.float32)
    return (produced * factor).astype(jnp.bfloat16)


def by_collectives(tokens, routes, gate_levels, w_gate, w_up, w_down):
    rows, width = tokens.shape
    devices = lax.axis_size("expert") * lax.axis_size("dp")
    me = lax.axis_index("expert") * lax.axis_size("dp") + lax.axis_index("dp")
    named = routes[:, :, None] == jnp.arange(devices, dtype=jnp.int32)[None, None, :]
    levels = gate_levels.astype(jnp.float32)
    weights = levels / jnp.sum(levels, axis=1, keepdims=True)
    spread = jnp.sum(jnp.where(named, weights[:, :, None], 0.0), axis=1)
    factors = lax.all_gather(spread, AXES, axis=0, tiled=False)
    mine = lax.dynamic_index_in_dim(factors, me, 2, keepdims=True)
    chunks = 2 if devices <= 16 else 8
    step = rows // chunks
    results = []
    for c in range(chunks):
        part = slice(c * step, (c + 1) * step)
        block = tokens[part]
        if devices > 16 and c > 0:
            block, _ = lax.optimization_barrier((block, results[-1]))
        x = lax.all_gather(block, AXES, axis=0, tiled=True)
        y = expert_part(x, mine[:, part].reshape(-1, 1), w_gate[0], w_up[0], w_down[0])
        results.append(lax.psum_scatter(y, AXES, scatter_dimension=0, tiled=True))
    return jnp.concatenate(results, axis=0)


LANES = 128
VMEM_ROOM = 56 * 1024 * 1024


def kernel(
    n, token_hbm, level_hbm, gate_hbm, up_hbm, down_hbm, out_ref,
    x, lev, w_gate, w_up, w_down, hid, own, sent, sib, run,
    load_sem, ring_send, ring_recv, pair_send, pair_recv,
    back_send, back_recv, run_send, run_recv,
    lev_send, lev_recv, lev_pair_send, lev_pair_recv,
):
    half_ring = n // 2
    rows, width = out_ref.shape
    piece = rows // 2
    expert = lax.axis_index("expert")
    core = lax.axis_index("dp")
    odd, rank = expert % 2, expert // 2
    place = rank + odd * (n - 1 - 2 * rank)

    def chip_at(p):
        return 2 * p + (p // half_ring) * (2 * n - 1 - 4 * p)

    right = {"expert": chip_at((place + 1) % n), "dp": core}
    left = {"expert": chip_at((place + n - 1) % n), "dp": core}
    other = {"expert": expert, "dp": 1 - core}
    ways = (right, left)
    number = expert * 2 + core

    loads = [
        pltpu.make_async_copy(src, dst, load_sem.at[i])
        for i, (src, dst) in enumerate(
            [
                (token_hbm, x.at[0, pl.ds(0, rows)]),
                (level_hbm, lev.at[0, 0]),
                (gate_hbm.at[0], w_gate),
                (up_hbm.at[0], w_up),
                (down_hbm.at[0], w_down),
            ]
        )
    ]
    for load in loads:
        load.start()

    barrier = pltpu.get_barrier_semaphore()
    for device in (right, left, other):
        pl.semaphore_signal(barrier, inc=1, device_id=device, device_id_type=pl.DeviceIdType.MESH)
    pl.semaphore_wait(barrier, 3)

    def slot_of(way, step):
        return step if way == 0 else (n - step) % n

    def remote(src, dst, send, recv, device):
        return pltpu.make_async_remote_copy(
            src_ref=src, dst_ref=dst, send_sem=send, recv_sem=recv,
            device_id=device, device_id_type=pl.DeviceIdType.MESH,
        )

    def ring_copy(way, step, part):
        rows_of = pl.ds(part * piece, piece)
        return remote(
            x.at[slot_of(way, step), rows_of], x.at[slot_of(way, step + 1), rows_of],
            ring_send.at[way, step, part], ring_recv.at[way, step, part], ways[way],
        )

    def level_copy(way, step):
        return remote(
            lev.at[slot_of(way, step), 0], lev.at[slot_of(way, step + 1), 0],
            lev_send.at[way, step], lev_recv.at[way, step], ways[way],
        )

    def level_travels(way, step):
        return step < half_ring - way

    def level_pair_copy(slot):
        return remote(
            lev.at[slot, 0], lev.at[slot, 1], lev_pair_send.at[slot], lev_pair_recv.at[slot], other
        )

    def upright(line):
        across = lax.broadcasted_iota(jnp.int32, (rows, rows), 1)
        down = lax.broadcasted_iota(jnp.int32, (rows, rows), 0)
        return jnp.sum(jnp.where(across == down, line, 0.0), axis=1, keepdims=True)

    def level_of(slot, side):
        table = lev[slot, side].astype(jnp.float32)
        chosen = lax.broadcasted_iota(jnp.int32, table.shape, 0) == number
        return upright(jnp.sum(jnp.where(chosen, table, 0.0), axis=0, keepdims=True))

    def pair_copy(slot, part):
        return remote(
            x.at[slot, pl.ds(part * piece, piece)], x.at[slot, pl.ds(rows + part * piece, piece)],
            pair_send.at[slot, part], pair_recv.at[slot, part], other,
        )

    def back_copy(slot):
        return remote(sent.at[slot], sib.at[slot], back_send.at[slot], back_recv.at[slot], other)

    def run_copy(way, hop, part):
        rows_of = pl.ds(part * piece, piece)
        return remote(
            run.at[way, hop, rows_of], run.at[way, hop + 1, rows_of],
            run_send.at[way, hop, part], run_recv.at[way, hop, part], ways[way],
        )

    def travels(way, step, part):
        return step < half_ring - 1 or part == way

    def compute(slot):
        level = jnp.concatenate([level_of(slot, side) for side in range(2)], axis=0)

        def hidden_part(i, carry):
            cols = pl.ds(pl.multiple_of(i * 256, 256), 256)
            tokens = x[slot]
            g = jnp.dot(tokens, w_gate[:, cols], preferred_element_type=jnp.float32)
            u = jnp.dot(tokens, w_up[:, cols], preferred_element_type=jnp.float32)
            hid[:, cols] = (g / (1.0 + jnp.exp(-g)) * u).astype(jnp.bfloat16)
            return carry

        lax.fori_loop(0, w_gate.shape[1] // 256, hidden_part, 0, unroll=True)

        def output_part(i, carry):
            cols = pl.ds(pl.multiple_of(i * 256, 256), 256)
            y = jnp.dot(hid[...], w_down[:, cols], preferred_element_type=jnp.float32) * level
            own[slot, :, cols] = y[:rows]
            sent[slot, :, cols] = y[rows:].astype(jnp.bfloat16)
            return carry

        lax.fori_loop(0, width // 256, output_part, 0, unroll=True)

    def slots_at(step):
        return [step] if step in (0, half_ring) else [step, n - step]

    def compute_step(step):
        for slot in slots_at(step):
            level_pair_copy(slot).wait_recv()
            for part in range(2):
                pair_copy(slot, part).wait_recv()
        first, count = step, len(slots_at(step))

        def body(i, carry):
            compute(first + i * (n - 2 * step))
            return carry

        lax.fori_loop(0, count, body, 0)
        for slot in slots_at(step):
            back_copy(slot).start()

    loads[0].wait()
    loads[1].wait()
    for way in range(2):
        level_copy(way, 0).start()
    level_pair_copy(0).start()
    for part in range(2):
        for way in range(2):
            ring_copy(way, 0, part if way == 0 else 1 - part).start()
    for part in range(2):
        pair_copy(0, part).start()
    for load in loads[2:]:
        load.wait()
    for step in range(1, half_ring + 1):
        compute_step(step - 1)
        for way in range(2):
            if level_travels(way, step - 1):
                level_copy(way, step - 1).wait_recv()
                if step < half_ring and level_travels(way, step):
                    level_copy(way, step).start()
                level_pair_copy(slot_of(way, step)).start()
        for order in range(2):
            for way in range(2):
                part = order if way == 0 else 1 - order
                if not travels(way, step - 1, part):
                    continue
                ring_copy(way, step - 1, part).wait_recv()
                if step < half_ring and travels(way, step, part):
                    ring_copy(way, step, part).start()
                pair_copy(slot_of(way, step), part).start()
    def here(slot, part):
        rows_of = pl.ds(part * piece, piece)
        return own[slot, rows_of] + sib[slot, rows_of].astype(jnp.float32)

    def pass_on(way, hop, part, arrives):
        slot = (n - (half_ring - hop)) % n if way == 0 else half_ring - hop
        rows_of = pl.ds(part * piece, piece)
        total = here(slot, part)
        if arrives:
            run_copy(way, hop - 1, part).wait_recv()
            total = total + run[way, hop, rows_of].astype(jnp.float32)
        run[way, hop, rows_of] = total.astype(jnp.bfloat16)
        run_copy(way, hop, part).start()

    for slot in slots_at(half_ring - 1):
        back_copy(slot).wait_recv()
    for way in range(2):
        pass_on(way, 1, 1 - way, False)
    compute_step(half_ring)
    back_copy(half_ring).wait_recv()
    for way in range(2):
        pass_on(way, 0, way, False)
    for way in range(2):
        pass_on(way, 1, way, True)
    for hop in range(2, half_ring):
        for slot in slots_at(half_ring - hop):
            back_copy(slot).wait_recv()
        for order in range(2):
            for way in range(2):
                pass_on(way, hop, 1 - way if order == 0 else way, True)
    share = 1.0 / upright(jnp.sum(lev[0, 0].astype(jnp.float32), axis=0, keepdims=True))
    back_copy(0).wait_recv()
    for order in range(2):
        for way in range(2):
            part = 1 - way if order == 0 else way
            run_copy(way, half_ring - 1, part).wait_recv()
    for part in range(2):
        rows_of = pl.ds(part * piece, piece)
        total = here(0, part)
        for way in range(2):
            total = total + run[way, half_ring, rows_of].astype(jnp.float32)
        out_ref[rows_of] = (total * share[part * piece : (part + 1) * piece]).astype(jnp.bfloat16)

    for way in range(2):
        for step in range(half_ring):
            if level_travels(way, step):
                level_copy(way, step).wait_send()
            for part in range(2):
                if travels(way, step, part):
                    ring_copy(way, step, part).wait_send()
        for hop in range(half_ring):
            for part in range(2):
                if hop > 0 or part == way:
                    run_copy(way, hop, part).wait_send()
    for slot in range(n):
        level_pair_copy(slot).wait_send()
        for part in range(2):
            pair_copy(slot, part).wait_send()
        back_copy(slot).wait_send()


def scratch_of(n, experts, rows, width, hidden):
    half_ring = n // 2
    arrays = [
        ((n, 2 * rows, width), jnp.bfloat16),
        ((n, 2, experts, rows), jnp.bfloat16),
        ((width, hidden), jnp.bfloat16),
        ((width, hidden), jnp.bfloat16),
        ((hidden, width), jnp.bfloat16),
        ((2 * rows, hidden), jnp.bfloat16),
        ((n, rows, width), jnp.float32),
        ((n, rows, width), jnp.bfloat16),
        ((n, rows, width), jnp.bfloat16),
        ((2, half_ring + 1, rows, width), jnp.bfloat16),
    ]
    total = sum(functools.reduce(lambda a, b: a * b, s) * jnp.dtype(t).itemsize for s, t in arrays)
    sems = [(5,), (2, half_ring, 2), (2, half_ring, 2), (n, 2), (n, 2), (n,), (n,),
            (2, half_ring, 2), (2, half_ring, 2), (2, half_ring), (2, half_ring), (n,), (n,)]
    shapes = [pltpu.VMEM(s, t) for s, t in arrays] + [pltpu.SemaphoreType.DMA(s) for s in sems]
    return shapes, total


def per_device(tokens, routes, gate_levels, w_gate, w_up, w_down):
    rows, width = tokens.shape
    hidden = w_gate.shape[2]
    n, cores = lax.axis_size("expert"), lax.axis_size("dp")
    experts = -(-n * cores // 16) * 16
    shapes, total = scratch_of(n, experts, rows, width, hidden)
    if total > VMEM_ROOM * 9 // 10 or n < 4 or n % 2 or cores != 2 or rows != LANES:
        return by_collectives(tokens, routes, gate_levels, w_gate, w_up, w_down)
    numbers = jnp.arange(experts, dtype=jnp.int32)[:, None, None]
    named = routes.T[None, :, :] == numbers
    levels = jnp.sum(jnp.where(named, gate_levels.T[None, :, :], 0), axis=1)
    any_space = pl.BlockSpec(memory_space=pl.ANY)
    return pl.pallas_call(
        functools.partial(kernel, n),
        out_shape=jax.ShapeDtypeStruct((rows, width), jnp.bfloat16),
        in_specs=[any_space] * 5,
        out_specs=pl.BlockSpec(memory_space=pltpu.VMEM),
        scratch_shapes=shapes,
        compiler_params=pltpu.CompilerParams(
            collective_id=0, has_side_effects=True, vmem_limit_bytes=VMEM_ROOM
        ),
        cost_estimate=pl.CostEstimate(
            flops=12 * n * rows * width * hidden,
            bytes_accessed=6 * width * hidden,
            transcendentals=2 * n * rows * hidden,
        ),
    )(tokens, levels.astype(jnp.bfloat16), w_gate, w_up, w_down)


def solution(mesh):
    token_spec = P(("groups", "expert", "dp"), None)
    weight_spec = P(("expert", "dp"), None, None)
    return jax.shard_map(
        per_device,
        mesh=mesh,
        in_specs=(token_spec,) * 3 + (weight_spec,) * 3,
        out_specs=token_spec,
        check_vma=False,
    )
```
